128 devices in a mesh: grp: 8 (over y, z_lo), seq: 16 (over z_hi, x, core).
Axes of the slice: x: 4, y: 4, z: 4 (z_hi: 2, z_lo: 2; z = z_hi * 2 + z_lo), core: 2. Of those that a mesh axis runs over, the one named last changes fastest.
Arguments:
- queries: bfloat16 [8, 4096, 4096], P('grp', 'seq'), may hold values from -240 to 240
- keys: bfloat16 [8, 4096, 1024], P('grp', 'seq'), may hold values from -6 to 6
- values: bfloat16 [8, 4096, 1024], P('grp', 'seq'), may hold values from -6 to 6
- block_mask: int32 [8, 32, 32], P('grp', 'seq'), may hold values 0 or 1
- counts: int32 [8], P('grp'), may hold values from 16 to 32
- owners: int32 [8, 32, 8, 1], P('grp', 'seq'), may hold values from 0 to 7; in each aligned block of 16 rows (0 to 15, 16 to 31, ..., all dimensions but the last counted through in order) at most 4 rows name the same one
Outputs:
- attended: bfloat16 [8, 4096, 4096], P('grp', 'seq')
- feedback: float32 [8, 16, 8, 4, 128], P('grp', 'seq')
The draws below stay inside these ranges and needn't reach their ends.
Inputs may be any that keep to these rules, and one draw needn't show every extreme that they name: `owners`: among the 16 rows of one run of 256 tokens, at most 4 name the same owner.
All inputs are finite; a program needn't handle non-finite values. No bound on the sum of `block_mask` on one device may be relied on, other than what follows from the above.
Results may differ from the reference program's by a relative error of at most 0.0075.
Values may be sent and summed in bfloat16 or wider, within the bound.
No kernel may reach another device: no remote copies, remote signals or barrier semaphores. Data moves between devices by JAX's collectives and lax.ppermute only.
A program may use at most 128 MiB of HBM per device.

```python
import math
import jax
import jax.numpy as jnp
import numpy as np
from jax import lax

HEADS = 32
KV_HEADS = 8
HEAD_DIM = 128
PLEN = 128
CAP = 4
GROUPS = 8
CTX = 4096
PASS_DEV = 2
PASSAGES = 32
N_SEQ = 16


def shared_keys(key):
    drawn = jax.random.normal(key, (GROUPS, PASSAGES, PLEN, KV_HEADS * HEAD_DIM), jnp.float32)
    level = jax.random.uniform(jax.random.fold_in(key, 11), (GROUPS, PASSAGES, 1, KV_HEADS * HEAD_DIM), jnp.float32, -0.7, 0.7)
    scaled = (drawn * jnp.exp(level)).reshape(GROUPS, CTX, KV_HEADS * HEAD_DIM)
    return jnp.clip(scaled, -6.0, 6.0)


def draw_keys(key, part):
    base_keys = shared_keys(key)
    return base_keys.astype(jnp.bfloat16)


def draw_queries(key, part):
    base_keys = shared_keys(key)
    key = jax.random.fold_in(key, 5)
    noise_key, shift_key, offset_key, pull_key = jax.random.split(key, 4)
    per_kv = HEADS // KV_HEADS
    drawn_values = jnp.clip(jax.random.normal(noise_key, (GROUPS, CTX, HEADS * HEAD_DIM), jnp.float32), -6.0, 6.0)
    index_shape = (GROUPS, CTX, KV_HEADS, per_kv)
    shift = jax.random.randint(shift_key, index_shape, 1, PASSAGES, jnp.int32)
    offset = jax.random.randint(offset_key, index_shape, 0, PLEN, jnp.int32)
    token = jnp.arange(CTX, dtype=jnp.int32)[None, :, None, None]
    partner = (token // PLEN + shift) % PASSAGES * PLEN + offset
    group_index = jnp.arange(GROUPS, dtype=jnp.int32)[:, None, None, None]
    head_index = jnp.arange(KV_HEADS, dtype=jnp.int32)[None, None, :, None]
    flat_index = (group_index * CTX + partner) * KV_HEADS + head_index
    partner_rows = base_keys.reshape(GROUPS * CTX * KV_HEADS, HEAD_DIM)[flat_index]
    pull = jax.random.uniform(pull_key, index_shape + (1,), jnp.float32, 0.4, 0.9)
    drawn_values = drawn_values + (pull * partner_rows).reshape(GROUPS, CTX, HEADS * HEAD_DIM)
    return drawn_values.astype(jnp.bfloat16)


def set_ends(values, stream_key, smallest, high):
    longest = values.shape.index(max(values.shape))
    spots = []
    for shift in (0, 1):
        where = [jax.random.randint(jax.random.fold_in(stream_key, axis), (), 0, length) for axis, length in enumerate(values.shape)]
        where[longest] = (where[longest] + shift) % values.shape[longest]
        spots.append(tuple(where))
    return values.at[spots[0]].set(smallest).at[spots[1]].set(high)


def block_scale(key, shape, pieces, least, largest):
    loudness = 1.0
    for position, shards_of in pieces:
        steps = jax.random.uniform(jax.random.fold_in(jax.random.fold_in(key, 6), position), (shards_of,), jnp.float32, least / len(pieces), largest / len(pieces))
        loudness = loudness * jnp.repeat(jnp.exp(steps), shape[position] // shards_of).reshape((-1,) + (1,) * (len(shape) - 1 - position))
    return loudness


def deal_out(rng, own, number, rows, count, top, limit, lean):
    ranking = jax.random.permutation(rng, count)
    heavy_load, ordinary = portions_of(count, rows * top, limit, lean, True), portions_of(count, rows * top, limit, lean, False)
    places = jnp.arange(count)

    def named(sizes, turn):
        used = int((sizes > 0).sum())
        fixed = max(1, used // 4)
        moved = fixed + (places - fixed + turn * (used - fixed)) % max(1, count - fixed)
        return jnp.zeros((count,), jnp.int32).at[ranking[jnp.where(places < fixed, places, moved)]].set(jnp.asarray(sizes, jnp.int32))

    sizes = jnp.where(number % 4 == 0, named(heavy_load, number // 4), named(ordinary, number - number // 4 - 1))
    mixed = jax.random.permutation(jax.random.fold_in(own, 3), count)
    giver, receiver = mixed[0:count // 2 * 2:2], mixed[1:count // 2 * 2:2]
    margin = jnp.minimum(sizes[giver] - 1, limit - sizes[receiver]) // 2
    margin = jnp.where((giver == ranking[0]) | (receiver == ranking[0]) | (sizes[receiver] == 0), 0, jnp.maximum(margin, 0))
    moved = jax.random.randint(jax.random.fold_in(own, 4), (count // 2,), 0, 1 << 20) % (margin + 1)
    sizes = sizes.at[giver].add(-moved).at[receiver].add(moved)
    labels = jnp.searchsorted(jnp.cumsum(sizes), jnp.arange(rows * top), side="right").astype(jnp.int32)
    grid = labels.reshape(top, rows).T
    grid = grid[jax.random.permutation(jax.random.fold_in(own, 1), rows)]
    turn = jax.random.randint(jax.random.fold_in(own, 2), (rows, 1), 0, top)
    return jnp.take_along_axis(grid, (jnp.arange(top)[None, :] + turn) % top, axis=1)


def portions_of(amount, total, reach, slope, full):
    weights = [(1 << 20) // math.isqrt(rank ** slope) + 1 for rank in range(1, amount + 1)]
    largest = reach if full else min(reach, max(-(-total // amount), total * weights[0] // sum(weights)))
    least = 1 if total - largest >= amount - 1 else 0
    given, spare = [largest] + [least] * (amount - 1), total - largest - least * (amount - 1)
    while spare > 0:
        candidates = [i for i in range(1, amount) if given[i] < largest] or [i for i in range(1, amount) if given[i] < reach]
        whole, budget = sum([weights[i] for i in candidates]), spare
        for i in candidates:
            extra = min(reach - given[i], max(1, budget * weights[i] // whole), spare)
            given[i] = given[i] + extra
            spare = spare - extra
    return np.array(given)


def centred(stream_key, shape, width, limit, cuts=(), held_as=jnp.bfloat16):
    array = jax.random.normal(stream_key, shape, jnp.float32) * width
    if len(cuts) > 0:
        array = block_scale(stream_key, shape, cuts, -0.22, 0.18) * array
    return jnp.clip(array, min=-limit, max=limit).astype(held_as)


def setup_inputs(seed: int = 0) -> dict:
    key_list = jax.random.split(jax.random.key(seed), 7)
    queries = draw_queries(jax.random.fold_in(key_list[6], 71), 0)
    keys = draw_keys(jax.random.fold_in(key_list[6], 71), 0)
    values = centred(key_list[2], (GROUPS, CTX, KV_HEADS * HEAD_DIM), 1.0, 6.0, ((0, 8), (1, 16)))
    block_mask = set_ends((jax.random.randint(key_list[3], (GROUPS, PASSAGES, PASSAGES), 0, 3) < 1).astype(jnp.int32), jax.random.fold_in(key_list[3], 1), 0, 1)
    counts = set_ends(jax.random.randint(key_list[4], (GROUPS,), PASSAGES // 2, PASSAGES + 1), jax.random.fold_in(key_list[4], 1), PASSAGES // 2, PASSAGES).astype(jnp.int32)
    owners_keys = jax.random.split(jax.random.fold_in(key_list[5], 1), GROUPS * PASSAGES * KV_HEADS // (PASS_DEV * KV_HEADS))
    owners_turns = jax.random.permutation(jax.random.fold_in(key_list[5], 3), GROUPS * PASSAGES * KV_HEADS // (PASS_DEV * KV_HEADS))
    owners = jax.vmap(lambda own, number: deal_out(jax.random.fold_in(key_list[5], 2), own, number, PASS_DEV * KV_HEADS, GROUPS, 1, CAP, 2))(owners_keys, owners_turns).reshape((GROUPS, PASSAGES, KV_HEADS, 1))
    return dict(queries=queries, keys=keys, values=values, block_mask=block_mask, counts=counts, owners=owners)


NEGATIVE = -1.0e30


def reference(queries, keys, values, block_mask, counts, owners):
    per_kv = HEADS // KV_HEADS
    block_rows = math.gcd(CTX, 512)

    def per_group(group_args):
        query_all, key_all, value_all, mask_group, live_count = group_args
        key_view = key_all.astype(jnp.float32).reshape(CTX, KV_HEADS, HEAD_DIM)
        value_view = value_all.astype(jnp.float32).reshape(CTX, KV_HEADS, HEAD_DIM)
        key_pass = jnp.arange(CTX, dtype=jnp.int32) // PLEN

        def per_block(mass_sum, block_index):
            offset = (block_index * block_rows).astype(jnp.int32)
            query_block = lax.dynamic_slice_in_dim(query_all, offset, block_rows, 0)
            query_block = query_block.astype(jnp.float32).reshape(block_rows, KV_HEADS, per_kv, HEAD_DIM)
            query_pass = (offset + jnp.arange(block_rows, dtype=jnp.int32)) // PLEN
            picked = mask_group[query_pass][:, key_pass]
            linked = (picked == 1) & (query_pass < live_count)[:, None] & (key_pass < live_count)[None, :]
            allowed = (query_pass[:, None] == key_pass[None, :]) | linked
            raw_scores = jnp.einsum("qgrd,kgd->grqk", query_block, key_view, precision=lax.Precision.HIGHEST) * (HEAD_DIM ** -0.5)
            scores = jnp.where(allowed[None, None], raw_scores, NEGATIVE)
            row_top = jnp.max(scores, axis=-1)
            exponent = jnp.where(allowed[None, None], jnp.exp(scores - row_top[..., None]), 0.0)
            row_total = jnp.sum(exponent, axis=-1)
            weights = exponent.astype(jnp.bfloat16)
            weights_wide = weights.astype(jnp.float32)
            output = jnp.einsum("grqk,kgd->qgrd", weights_wide, value_view, precision=lax.Precision.HIGHEST)
            output = output / jnp.transpose(row_total, (2, 0, 1))[..., None]
            mass_sum = mass_sum + jnp.sum(weights_wide * (1.0 / row_total)[..., None], axis=(1, 2))
            return mass_sum, output.reshape(block_rows, HEADS * HEAD_DIM).astype(jnp.bfloat16)

        mass_sum, attended_blocks = lax.scan(per_block, jnp.zeros((KV_HEADS, CTX), jnp.float32), jnp.arange(CTX // block_rows, dtype=jnp.int32))
        return attended_blocks.reshape(CTX, HEADS * HEAD_DIM), mass_sum / per_kv

    attended, attention_mass = lax.map(per_group, (queries, keys, values, block_mask, counts))
    rows_dev = PASS_DEV * KV_HEADS
    mass_rows = attention_mass.reshape(GROUPS, KV_HEADS, N_SEQ, PASS_DEV, PLEN)
    mass_rows = jnp.transpose(mass_rows, (0, 2, 3, 1, 4)).reshape(GROUPS, N_SEQ, rows_dev, PLEN)
    destination = owners.reshape(GROUPS, N_SEQ, rows_dev)
    onehot = (destination[..., None] == jnp.arange(GROUPS, dtype=jnp.int32)).astype(jnp.int32)
    slot_index = jnp.sum((jnp.cumsum(onehot, axis=2) - 1) * onehot, axis=3)
    selection = onehot[..., None] * (slot_index[..., None, None] == jnp.arange(CAP, dtype=jnp.int32)).astype(jnp.int32)
    feedback = jnp.einsum("gsroc,gsrt->osgct", selection.astype(jnp.float32), mass_rows, precision=lax.Precision.HIGHEST)
    return attended, feedback
```

```python
import functools
import math

import jax
import jax.numpy as jnp
from jax import lax
from jax.experimental import pallas as pl
from jax.experimental.pallas import tpu as pltpu
from jax.sharding import Mesh, PartitionSpec as P

D = 128
PASSAGES = 32
BLOCKS = 16
CAP = 4
REPEAT = 4
WIDE = REPEAT * D
SCALE2 = (D**-0.5) * math.log2(math.e)
LARGE = 2.0**80
SEQ = ("zh", "x", "core")
REAL, COUNT, OWN, FAR, SRC = 64, 66, 68, 70, 80
SPLIT = (8,)
CALLS = ((8,),)
EXTRA = 32
VMEM = 56


def matmul(a, b):
    return lax.dot_general(a, b, (((1,), (0,)), ((), ())), preferred_element_type=jnp.float32)


def rows_at(i, n=1):
    return pl.ds(pl.multiple_of(i * D, D), n * D)


def each(n, body, start=0):
    def step(i, carry):
        body(i)
        return carry

    lax.fori_loop(start, n, step, 0)


def chunks(n, body):
    each(n // 8, lambda i: body(i * 8, 8))

    @pl.when(n % 8 > 0)
    def _():
        body(n // 8 * 8, 4)


def weights_kernel(heads, offset, table, q_ref, *rest):
    kblocks = rest[:BLOCKS]
    p_ref, inv_ref, mass_ref, kbuf, pbuf, qt, total, ksem, psem = rest[BLOCKS:]
    h = pl.program_id(0)

    @pl.when(h == 0)
    def _():
        for hh in range(heads):
            for b in range(BLOCKS):
                pltpu.make_async_copy(
                    kblocks[b].at[pl.ds(0, 2 * D), pl.ds((offset + hh) * D, D)],
                    kbuf.at[hh, rows_at(table[SRC + b] * 2, 2)],
                    ksem.at[hh],
                ).start()

    pltpu.make_async_copy(kbuf.at[h], kbuf.at[h], ksem.at[h]).wait()
    mass_ref[...] = jnp.zeros_like(mass_ref)

    def pcopy(hh, qp, i):
        return pltpu.make_async_copy(
            pbuf.at[qp, rows_at(i * 4, 4)], p_ref.at[hh, qp, rows_at(i * 4, 4)], psem.at[qp, i]
        )

    for qp in range(2):
        n = table[COUNT + qp]
        for r in range(REPEAT):
            qt[qp, :, r * D : (r + 1) * D] = q_ref[qp * D : (qp + 1) * D, r * D : (r + 1) * D].T

        @pl.when(h > 0)
        def _():
            each(n // 4, lambda i: pcopy(h - 1, qp, i).wait())

        def key_at(i):
            return kbuf[h, rows_at(table[qp * PASSAGES + i]), :]

        def fill(top):
            def part(first, count):
                k = jnp.concatenate([key_at(first + u) for u in range(count)], axis=0)
                s = matmul(k, qt[qp]) * SCALE2
                acc = total[qp]
                for u in range(count):
                    unused = jnp.where(first + u < table[REAL + qp], 0.0, 1e30)
                    w = jnp.exp2(s[u * D : (u + 1) * D] - (top + unused))
                    pbuf[qp, rows_at(first + u), :] = w.astype(jnp.bfloat16)
                    acc = acc + jnp.sum(w.reshape(D // 8, 8, WIDE), axis=0)
                total[qp] = acc

            total[qp] = jnp.zeros((8, WIDE), jnp.float32)
            chunks(n, part)
            total[qp] = jnp.broadcast_to(jnp.sum(total[qp], axis=0, keepdims=True), (8, WIDE))

        own = jnp.max(
            matmul(kbuf[h, rows_at(table[OWN + qp]), :], qt[qp]), axis=0, keepdims=True
        )
        fill(own * SCALE2)

        @pl.when(jnp.max(total[qp]) > LARGE)
        def _():
            def higher(i, top):
                return jnp.maximum(
                    top, jnp.max(matmul(key_at(i), qt[qp]), axis=0, keepdims=True)
                )

            fill(lax.fori_loop(0, n, higher, own) * SCALE2)

        each(n // 4, lambda i: pcopy(h, qp, i).start())
        inv = 1.0 / total[qp]
        inv_ref[0, qp] = inv

        def mass_part(first, count):
            w = pbuf[qp, rows_at(first, count), :].astype(jnp.float32) * inv[0:1]
            w = w[:, :D] + w[:, D : 2 * D] + w[:, 2 * D : 3 * D] + w[:, 3 * D :]
            for u in range(count):
                row = jnp.sum(w[u * D : (u + 1) * D].T, axis=0, keepdims=True)
                j = table[qp * PASSAGES + first + u]
                mass_ref[0, pl.ds(j, 1), :] += row

        chunks(n, mass_part)

    @pl.when(h == heads - 1)
    def _():
        for qp in range(2):
            each(table[COUNT + qp] // 4, lambda i: pcopy(h, qp, i).wait())


def weights_call(q, kblocks, table, first_head, offset, heads):
    grid_spec = pltpu.PrefetchScalarGridSpec(
        num_scalar_prefetch=1,
        grid=(heads,),
        in_specs=[pl.BlockSpec((2 * D, WIDE), lambda h, *_: (0, h + first_head))]
        + [pl.BlockSpec(memory_space=pl.ANY)] * BLOCKS,
        out_specs=[
            pl.BlockSpec(memory_space=pl.ANY),
            pl.BlockSpec((1, 2, 8, WIDE), lambda h, *_: (h, 0, 0, 0)),
            pl.BlockSpec((1, PASSAGES, D), lambda h, *_: (h, 0, 0)),
        ],
        scratch_shapes=[
            pltpu.VMEM((heads, PASSAGES * D, D), jnp.bfloat16),
            pltpu.VMEM((2, PASSAGES * D, WIDE), jnp.bfloat16),
            pltpu.VMEM((2, D, WIDE), jnp.bfloat16),
            pltpu.VMEM((2, 8, WIDE), jnp.float32),
            pltpu.SemaphoreType.DMA((heads,)),
            pltpu.SemaphoreType.DMA((2, PASSAGES // 4)),
        ],
    )
    return pl.pallas_call(
        functools.partial(weights_kernel, heads, offset),
        grid_spec=grid_spec,
        out_shape=[
            jax.ShapeDtypeStruct((heads, 2, PASSAGES * D, WIDE), jnp.bfloat16),
            jax.ShapeDtypeStruct((heads, 2, 8, WIDE), jnp.float32),
            jax.ShapeDtypeStruct((heads, PASSAGES, D), jnp.float32),
        ],
        compiler_params=pltpu.CompilerParams(vmem_limit_bytes=VMEM << 20),
        cost_estimate=pl.CostEstimate(
            flops=heads * 5_000_000_000, bytes_accessed=heads * 4_000_000, transcendentals=0
        ),
        name="weights",
    )(table, q, *kblocks)


def attend_kernel(heads, table, *rest):
    parts = len(heads)
    total = sum(heads)
    p_refs, inv_ref, vblocks = rest[:parts], rest[parts], rest[parts + 1 : parts + 1 + BLOCKS]
    o_ref, vbuf, pbuf, acc, vsem, psem = rest[-6:]
    h = pl.program_id(0)

    def pcopy(ref, hh, qp, i, slot):
        return pltpu.make_async_copy(
            ref.at[hh, qp, rows_at(i * 4, 4)], pbuf.at[slot, qp, rows_at(i * 4, 4)], psem.at[slot, qp, i]
        )

    def fetch(hh, qp, slot):
        lo = 0
        for ref, n in zip(p_refs, heads):

            @pl.when((hh >= lo) & (hh < lo + n))
            def _():
                each(table[COUNT + qp] // 4, lambda i: pcopy(ref, hh - lo, qp, i, slot).start())

            lo += n

    @pl.when(h == 0)
    def _():
        fetch(0, 0, 0)
        fetch(0, 1, 0)
        for hh in range(total):
            for b in range(BLOCKS):
                for p in range(2):
                    pltpu.make_async_copy(
                        vblocks[b].at[pl.ds(hh * D, D), pl.ds(p * D, D)],
                        vbuf.at[hh, rows_at(table[SRC + b] * 2 + p)],
                        vsem.at[hh],
                    ).start()

    slot = lax.rem(h, 2)

    @pl.when(h < total - 1)
    def _():
        fetch(h + 1, 0, 1 - slot)
        fetch(h + 1, 1, 1 - slot)

    pltpu.make_async_copy(vbuf.at[h], vbuf.at[h], vsem.at[h]).wait()
    for qp in range(2):
        n = table[COUNT + qp]
        acc[...] = jnp.zeros_like(acc)

        def part(first, count):
            for u in range(0, count, 4):
                pcopy(p_refs[0], 0, qp, (first + u) // 4, slot).wait()
            v = jnp.concatenate(
                [vbuf[h, rows_at(table[qp * PASSAGES + first + u]), :] for u in range(count)], axis=1
            )
            acc[...] += matmul(v, pbuf[slot, qp, rows_at(first, count), :])

        chunks(n, part)

        o = acc[...] * inv_ref[0, qp, 0:1, :]
        for r in range(REPEAT):
            o_ref[qp * D : (qp + 1) * D, r * D : (r + 1) * D] = (
                o[:, r * D : (r + 1) * D].T.astype(jnp.bfloat16)
            )


def attend_call(vblocks, weights, invs, table):
    heads = tuple(w.shape[0] for w in weights)
    total = sum(heads)
    inv = jnp.concatenate(invs, axis=0)
    grid_spec = pltpu.PrefetchScalarGridSpec(
        num_scalar_prefetch=1,
        grid=(total,),
        in_specs=[pl.BlockSpec(memory_space=pl.ANY)] * len(weights)
        + [pl.BlockSpec((1, 2, 8, WIDE), lambda h, *_: (h, 0, 0, 0))]
        + [pl.BlockSpec(memory_space=pl.ANY)] * BLOCKS,
        out_specs=pl.BlockSpec((2 * D, WIDE), lambda h, *_: (0, h)),
        scratch_shapes=[
            pltpu.VMEM((total, PASSAGES * D, D), jnp.bfloat16),
            pltpu.VMEM((2, 2, PASSAGES * D, WIDE), jnp.bfloat16),
            pltpu.VMEM((D, WIDE), jnp.float32),
            pltpu.SemaphoreType.DMA((total,)),
            pltpu.SemaphoreType.DMA((2, 2, PASSAGES // 4)),
        ],
    )
    return pl.pallas_call(
        functools.partial(attend_kernel, heads),
        grid_spec=grid_spec,
        out_shape=jax.ShapeDtypeStruct((2 * D, total * WIDE), jnp.bfloat16),
        compiler_params=pltpu.CompilerParams(vmem_limit_bytes=VMEM << 20),
        cost_estimate=pl.CostEstimate(
            flops=total * 2_000_000_000, bytes_accessed=total * 4_000_000, transcendentals=0
        ),
        name="attend",
    )(table, *weights, inv, *vblocks)


def step_x(block, distance):
    n = lax.axis_size("x")
    return lax.ppermute(block, "x", [(i, (i + distance) % n) for i in range(n)])


def swap(block, axis):
    return lax.ppermute(block, axis, [(0, 1), (1, 0)])


def after(block, *others):
    return lax.optimization_barrier((block, *others))[0]


class Gather:
    OFFSETS = [(0, 0), (1, 0), (0, -1), (0, 1), (0, 2), (1, -1), (1, 1), (1, 2)]

    def __init__(self, block):
        self.block = block

    def first(self, *others):
        block = after(self.block, *others) if others else self.block
        self.block = block
        self.far = swap(block, "zh")
        self.right, self.left, self.opposite = (step_x(block, n) for n in (1, -1, 2))
        return self.far, self.right, self.left, self.opposite

    def first_arrived(self):
        return self.far, self.right, self.left, self.opposite

    def second(self, *others):
        if others:
            self.far = after(self.far, *others)
            self.opposite = after(self.opposite, *others)
        self.far_right, self.far_left = step_x(self.far, 1), step_x(self.far, -1)
        self.far_opposite = swap(self.opposite, "zh")
        return self.far_right, self.far_left, self.far_opposite

    def blocks(self, *others):
        got = [
            self.block,
            self.far,
            self.right,
            self.left,
            self.opposite,
            self.far_right,
            self.far_left,
            self.far_opposite,
        ]
        if others:
            got = list(lax.optimization_barrier((*got, *others))[: len(got)])
        return got + [swap(b, "core") for b in got]


def turn_kernel(x_ref, o_ref):
    for i in range(x_ref.shape[1] // D):
        o_ref[i * D : (i + 1) * D, :] = x_ref[:, i * D : (i + 1) * D].T


def turn_call(x):
    return pl.pallas_call(
        turn_kernel, out_shape=jax.ShapeDtypeStruct(x.shape[::-1], x.dtype), name="turn"
    )(x)


def route_kernel(table, mass_ref, *rest):
    kblocks = rest[:BLOCKS]
    out_ref, named, sem = rest[BLOCKS:]
    for b in range(BLOCKS):
        pltpu.make_async_copy(
            kblocks[b].at[pl.ds(2 * D, 16), pl.ds(0, D)], named.at[table[SRC + b]], sem
        ).start()
    pltpu.make_async_copy(named, named, sem).wait()
    r = lax.broadcasted_iota(jnp.int32, (16, D), 0)
    lane = lax.broadcasted_iota(jnp.int32, (16, D), 1)
    owner_of = lax.broadcasted_iota(jnp.int32, (32, 16), 0) // CAP
    slot_of = lax.broadcasted_iota(jnp.int32, (32, 16), 0) % CAP
    for s in range(BLOCKS):
        own = named[s, 0:1, :].astype(jnp.float32)
        wide = jnp.broadcast_to(own, (16, D))
        tall = jnp.sum(jnp.where(r == lane, wide, 0.0), axis=1, keepdims=True)
        earlier = jnp.where((wide == tall) & (r < lane), 1.0, 0.0)
        slot = jnp.sum(earlier, axis=0, keepdims=True)
        pick = (own[:, :16] == owner_of.astype(jnp.float32)) & (
            slot[:, :16] == slot_of.astype(jnp.float32)
        )
        rows = jnp.concatenate([mass_ref[:, 2 * s, :], mass_ref[:, 2 * s + 1, :]], axis=0)
        out = lax.dot_general(
            pick.astype(jnp.float32),
            rows * (1.0 / REPEAT),
            (((1,), (0,)), ((), ())),
            precision=lax.Precision.HIGHEST,
            preferred_element_type=jnp.float32,
        )
        out_ref[:, s] = out.reshape(8, CAP, D)


def route_call(mass, kblocks, table):
    grid_spec = pltpu.PrefetchScalarGridSpec(
        num_scalar_prefetch=1,
        grid=(1,),
        in_specs=[pl.BlockSpec(mass.shape, lambda i, *_: (0, 0, 0))]
        + [pl.BlockSpec(memory_space=pl.ANY)] * BLOCKS,
        out_specs=pl.BlockSpec((8, BLOCKS, CAP, D), lambda i, *_: (0, 0, 0, 0)),
        scratch_shapes=[
            pltpu.VMEM((BLOCKS, 16, D), jnp.bfloat16),
            pltpu.SemaphoreType.DMA,
        ],
    )
    return pl.pallas_call(
        route_kernel,
        grid_spec=grid_spec,
        out_shape=jax.ShapeDtypeStruct((8, BLOCKS, CAP, D), jnp.float32),
        compiler_params=pltpu.CompilerParams(vmem_limit_bytes=VMEM << 20),
        name="route",
    )(table, mass, *kblocks)


def body(queries, keys, values, block_mask, counts, owners):
    kv_heads = keys.shape[2] // D
    q, k, v = queries[0], keys[0], values[0]
    zh, x, core = lax.axis_index("zh"), lax.axis_index("x"), lax.axis_index("core")
    me = zh * 8 + x * 2 + core

    cuts = [sum(SPLIT[:i]) for i in range(len(SPLIT) + 1)]
    kparts = [k[:, lo * D : hi * D] for lo, hi in zip(cuts, cuts[1:])]
    extra = jnp.pad(
        owners.reshape(1, 2 * kv_heads).astype(jnp.bfloat16),
        ((0, EXTRA - 1), (0, SPLIT[0] * D - 2 * kv_heads)),
    )
    kparts[0] = jnp.concatenate([kparts[0], extra], axis=0)
    kg = [Gather(part) for part in kparts]

    query_pass = me * 2 + jnp.arange(2, dtype=jnp.int32)
    key_pass = jnp.arange(PASSAGES, dtype=jnp.int32)
    live = counts[0]
    allowed = (query_pass[:, None] == key_pass) | (
        (block_mask[0] == 1) & (query_pass < live)[:, None] & (key_pass < live)
    )
    place = jnp.cumsum(allowed.astype(jnp.int32), axis=1) - 1
    real = jnp.sum(allowed.astype(jnp.int32), axis=1)
    hit = allowed[:, None, :] & (place[:, None, :] == key_pass[None, :, None])
    idx = jnp.sum(jnp.where(hit, key_pass, 0), axis=2).astype(jnp.int32)
    cnt = (real + 3) // 4 * 4
    src = jnp.stack(
        [
            ((zh + a) % 2) * 8 + ((x + b) % 4) * 2 + (core + c) % 2
            for c in range(2)
            for a, b in Gather.OFFSETS
        ]
    ).astype(jnp.int32)
    planes = jnp.stack([zh, 1 - zh]).astype(jnp.int32)
    pad = jnp.zeros((SRC - FAR - 2,), jnp.int32)
    table = jnp.concatenate([idx.reshape(-1), real, cnt, query_pass, planes, pad, src])

    (g,) = kg
    g.first()
    vt = turn_call(v)
    arrived = g.second(table, vt)
    vg = Gather(vt)
    vg.first(*arrived)

    parts = []
    kfirst = None
    for c, heads in enumerate(SPLIT):
        blocks = kg[c].blocks(*([parts[-1][1]] if parts else []))
        if c == 0:
            kfirst = blocks
        lo = 0
        for n in CALLS[c]:
            qd = q if not parts else after(q, parts[-1][1])
            parts.append(weights_call(qd, blocks, table, cuts[c] + lo, lo, n))
            lo += n
    vg.second(parts[-1][1])
    mass = jnp.concatenate([p[2] for p in parts], axis=0)

    owner_count = lax.axis_size("grp")
    outgoing = route_call(mass, kfirst, table).reshape(owner_count * BLOCKS, CAP, D)
    vblocks = vg.blocks(outgoing)
    incoming = lax.all_to_all(outgoing, ("grp",) + SEQ, split_axis=0, concat_axis=0, tiled=True)
    attended = attend_call(vblocks, [p[0] for p in parts], [p[1] for p in parts], table)
    incoming, attended = lax.optimization_barrier((incoming, attended))
    feedback = jnp.sum(incoming.reshape(owner_count, BLOCKS, CAP, D), axis=1)
    return attended[None], feedback[None, None]


def solution(mesh):
    fine = Mesh(mesh.devices.reshape(-1, 2, 4, 2), ("grp",) + SEQ)
    rows = P("grp", SEQ, None)
    in_specs = (rows, rows, rows, rows, P("grp"), P("grp", SEQ, None, None))
    out_specs = (rows, P("grp", SEQ, None, None, None))
    return jax.shard_map(
        body, mesh=fine, in_specs=in_specs, out_specs=out_specs, check_vma=False
    )
```

```python
import functools
import math

import jax
import jax.numpy as jnp
from jax import lax
from jax.experimental import pallas as pl
from jax.experimental.pallas import tpu as pltpu
from jax.sharding import Mesh, PartitionSpec as P

D = 128
PASSAGES = 32
BLOCKS = 16
CAP = 4
REPEAT = 4
WIDE = REPEAT * D
SCALE2 = (D**-0.5) * math.log2(math.e)
LARGE = 2.0**80
SEQ = ("zh", "x", "core")
REAL, COUNT, OWN, FAR, SRC = 64, 66, 68, 70, 80
CALLS = (5, 3)
EXTRA = 16
VMEM = 56


def matmul(a, b):
    return lax.dot_general(a, b, (((1,), (0,)), ((), ())), preferred_element_type=jnp.float32)


def rows_at(i, n=1):
    return pl.ds(pl.multiple_of(i * D, D), n * D)


def each(n, body, start=0):
    def step(i, carry):
        body(i)
        return carry

    lax.fori_loop(start, n, step, 0)


def chunks(n, body):
    each(n // 16, lambda i: body(i * 16, 16))

    @pl.when(n % 16 >= 8)
    def _():
        body(n // 16 * 16, 8)

    @pl.when(n % 8 > 0)
    def _():
        body(n // 8 * 8, 4)


def weights_kernel(heads, offset, table, q_ref, *rest):
    kblocks = rest[:BLOCKS]
    p_ref, inv_ref, mass_ref, kbuf, pbuf, qt, total, ksem, psem = rest[BLOCKS:]
    h = pl.program_id(0)

    def whole(cols, i):
        return pltpu.make_async_copy(kbuf.at[:, cols], kbuf.at[:, cols], ksem.at[i])

    spans = [pl.ds(0, D), pl.ds(D, (heads - 1) * D)][: min(heads, 2)]

    @pl.when(h == 0)
    def _():
        for i, cols in enumerate(spans):
            for b in range(BLOCKS):
                pltpu.make_async_copy(
                    kblocks[b].at[pl.ds(0, 2 * D), pl.ds(offset * D + cols.start, cols.size)],
                    kbuf.at[rows_at(table[SRC + b] * 2, 2), cols],
                    ksem.at[i],
                ).start()
        whole(spans[0], 0).wait()

    if heads > 1:

        @pl.when(h == 1)
        def _():
            whole(spans[1], 1).wait()

    mine = pl.ds(pl.multiple_of(h * D, D), D)
    mass_ref[...] = jnp.zeros_like(mass_ref)

    def pcopy(hh, qp, i):
        slot = lax.rem(hh, 2)
        return pltpu.make_async_copy(
            pbuf.at[slot, qp, rows_at(i * 4, 4)],
            p_ref.at[hh, qp, rows_at(i * 4, 4)],
            psem.at[slot, qp, i],
        )

    counts = [table[COUNT + qp] for qp in range(2)]

    mine_p = pbuf.at[lax.rem(h, 2)]

    def drain(hh):
        for qp in range(2):
            each(counts[qp] // 4, lambda i: pcopy(hh, qp, i).wait())

    @pl.when(h > 1)
    def _():
        drain(h - 2)

    def key_at(qp, i):
        return kbuf[rows_at(table[qp * PASSAGES + i]), mine]

    def fill(qp, top):
        def part(first, count):
            k = jnp.concatenate([key_at(qp, first + u) for u in range(count)], axis=0)
            s = matmul(k, qt[qp]) * SCALE2
            acc = total[qp]
            for u in range(count):
                unused = jnp.where(first + u < table[REAL + qp], 0.0, 1e30)
                w = jnp.exp2(s[u * D : (u + 1) * D] - (top + unused))
                mine_p[qp, rows_at(first + u), :] = w.astype(jnp.bfloat16)
                acc = acc + jnp.sum(w.reshape(D // 8, 8, WIDE), axis=0)
            total[qp] = acc
            for u in range(0, count, 4):
                pcopy(h, qp, (first + u) // 4).start()

        total[qp] = jnp.zeros((8, WIDE), jnp.float32)
        chunks(counts[qp], part)

    def summed(qp):
        return jnp.broadcast_to(jnp.sum(total[qp], axis=0, keepdims=True), (8, WIDE))

    for qp in range(2):
        for r in range(REPEAT):
            qt[qp, :, r * D : (r + 1) * D] = q_ref[qp * D : (qp + 1) * D, r * D : (r + 1) * D].T
    own = [
        jnp.max(
            matmul(kbuf[rows_at(table[OWN + qp]), mine], qt[qp]), axis=0, keepdims=True
        )
        for qp in range(2)
    ]
    for qp in range(2):
        fill(qp, own[qp] * SCALE2)

    @pl.when(jnp.max(jnp.maximum(summed(0), summed(1))) > LARGE)
    def _():
        drain(h)
        for qp in range(2):

            def higher(i, top):
                return jnp.maximum(
                    top, jnp.max(matmul(key_at(qp, i), qt[qp]), axis=0, keepdims=True)
                )

            fill(qp, lax.fori_loop(0, counts[qp], higher, own[qp]) * SCALE2)

    invs = [1.0 / summed(qp) for qp in range(2)]
    for qp in range(2):
        inv_ref[0, qp] = invs[qp]

        def mass_part(first, count):
            w = mine_p[qp, rows_at(first, count), :].astype(jnp.float32) * invs[qp][0:1]
            w = w[:, :D] + w[:, D : 2 * D] + w[:, 2 * D : 3 * D] + w[:, 3 * D :]
            for u in range(count):
                row = jnp.sum(w[u * D : (u + 1) * D].T, axis=0, keepdims=True)
                j = table[qp * PASSAGES + first + u]
                mass_ref[0, pl.ds(j, 1), :] += row

        chunks(counts[qp], mass_part)

    @pl.when(h == heads - 1)
    def _():
        if heads > 1:
            drain(h - 1)
        drain(h)


def weights_call(q, kblocks, table, first_head, offset, heads):
    grid_spec = pltpu.PrefetchScalarGridSpec(
        num_scalar_prefetch=1,
        grid=(heads,),
        in_specs=[pl.BlockSpec((2 * D, WIDE), lambda h, *_: (0, h + first_head))]
        + [pl.BlockSpec(memory_space=pl.ANY)] * BLOCKS,
        out_specs=[
            pl.BlockSpec(memory_space=pl.ANY),
            pl.BlockSpec((1, 2, 8, WIDE), lambda h, *_: (h, 0, 0, 0)),
            pl.BlockSpec((1, PASSAGES, D), lambda h, *_: (h, 0, 0)),
        ],
        scratch_shapes=[
            pltpu.VMEM((PASSAGES * D, heads * D), jnp.bfloat16),
            pltpu.VMEM((2, 2, PASSAGES * D, WIDE), jnp.bfloat16),
            pltpu.VMEM((2, D, WIDE), jnp.bfloat16),
            pltpu.VMEM((2, 8, WIDE), jnp.float32),
            pltpu.SemaphoreType.DMA((2,)),
            pltpu.SemaphoreType.DMA((2, 2, PASSAGES // 4)),
        ],
    )
    return pl.pallas_call(
        functools.partial(weights_kernel, heads, offset),
        grid_spec=grid_spec,
        out_shape=[
            jax.ShapeDtypeStruct((heads, 2, PASSAGES * D, WIDE), jnp.bfloat16),
            jax.ShapeDtypeStruct((heads, 2, 8, WIDE), jnp.float32),
            jax.ShapeDtypeStruct((heads, PASSAGES, D), jnp.float32),
        ],
        compiler_params=pltpu.CompilerParams(vmem_limit_bytes=VMEM << 20),
        cost_estimate=pl.CostEstimate(
            flops=heads * 5_000_000_000, bytes_accessed=heads * 4_000_000, transcendentals=0
        ),
        name="weights",
    )(table, q, *kblocks)


def attend_kernel(heads, table, *rest):
    parts = len(heads)
    total = sum(heads)
    p_refs, inv_refs = rest[:parts], rest[parts : 2 * parts]
    vblocks = rest[2 * parts : 2 * parts + BLOCKS]
    o_ref, vbuf, pbuf, acc, vsem, psem = rest[-6:]
    h = pl.program_id(0)

    def pcopy(ref, hh, qp, i, slot):
        return pltpu.make_async_copy(
            ref.at[hh, qp, rows_at(i * 4, 4)], pbuf.at[slot, qp, rows_at(i * 4, 4)], psem.at[slot, qp, i]
        )

    def fetch(hh, qp, slot):
        lo = 0
        for ref, n in zip(p_refs, heads):

            @pl.when((hh >= lo) & (hh < lo + n))
            def _():
                each(table[COUNT + qp] // 4, lambda i: pcopy(ref, hh - lo, qp, i, slot).start())

            lo += n

    def values(hh):
        rows = pl.ds(pl.multiple_of(hh * D, D), D)
        for b in range(BLOCKS):
            pltpu.make_async_copy(
                vblocks[b].at[rows], vbuf.at[table[SRC + b], rows], vsem.at[hh]
            ).start()

    @pl.when(h == 0)
    def _():
        fetch(0, 0, 0)
        values(0)
        fetch(0, 1, 0)

    slot = lax.rem(h, 2)

    @pl.when(h < total - 1)
    def _():
        fetch(h + 1, 0, 1 - slot)
        values(h + 1)
        fetch(h + 1, 1, 1 - slot)

    mine = pl.ds(pl.multiple_of(h * D, D), D)
    pltpu.make_async_copy(vbuf.at[:, mine], vbuf.at[:, mine], vsem.at[h]).wait()

    def value_at(j):
        return vbuf[j // 2, mine, rows_at(j % 2)]

    for qp in range(2):
        n = table[COUNT + qp]
        acc[...] = jnp.zeros_like(acc)

        def part(first, count):
            for u in range(0, count, 4):
                pcopy(p_refs[0], 0, qp, (first + u) // 4, slot).wait()
            v = jnp.concatenate(
                [value_at(table[qp * PASSAGES + first + u]) for u in range(count)], axis=1
            )
            acc[...] += matmul(v, pbuf[slot, qp, rows_at(first, count), :])

        chunks(n, part)

        lo = heads[0]
        inv = inv_refs[0][0, qp, 0:1, :]
        for ref, n in zip(inv_refs[1:], heads[1:]):
            inv = jnp.where(h >= lo, ref[0, qp, 0:1, :], inv)
            lo += n
        o = acc[...] * inv
        for r in range(REPEAT):
            o_ref[qp * D : (qp + 1) * D, r * D : (r + 1) * D] = (
                o[:, r * D : (r + 1) * D].T.astype(jnp.bfloat16)
            )


def attend_call(vblocks, weights, invs, table):
    heads = tuple(w.shape[0] for w in weights)
    total = sum(heads)
    firsts = [sum(heads[:i]) for i in range(len(heads))]

    def inv_spec(lo, n):
        return pl.BlockSpec((1, 2, 8, WIDE), lambda h, *_: (jnp.clip(h - lo, 0, n - 1), 0, 0, 0))

    grid_spec = pltpu.PrefetchScalarGridSpec(
        num_scalar_prefetch=1,
        grid=(total,),
        in_specs=[pl.BlockSpec(memory_space=pl.ANY)] * len(weights)
        + [inv_spec(lo, n) for lo, n in zip(firsts, heads)]
        + [pl.BlockSpec(memory_space=pl.ANY)] * BLOCKS,
        out_specs=pl.BlockSpec((2 * D, WIDE), lambda h, *_: (0, h)),
        scratch_shapes=[
            pltpu.VMEM((BLOCKS, total * D, 2 * D), jnp.bfloat16),
            pltpu.VMEM((2, 2, PASSAGES * D, WIDE), jnp.bfloat16),
            pltpu.VMEM((D, WIDE), jnp.float32),
            pltpu.SemaphoreType.DMA((total,)),
            pltpu.SemaphoreType.DMA((2, 2, PASSAGES // 4)),
        ],
    )
    return pl.pallas_call(
        functools.partial(attend_kernel, heads),
        grid_spec=grid_spec,
        out_shape=jax.ShapeDtypeStruct((2 * D, total * WIDE), jnp.bfloat16),
        compiler_params=pltpu.CompilerParams(vmem_limit_bytes=VMEM << 20),
        cost_estimate=pl.CostEstimate(
            flops=total * 2_000_000_000, bytes_accessed=total * 4_000_000, transcendentals=0
        ),
        name="attend",
    )(table, *weights, *invs, *vblocks)


def step_x(block, distance):
    n = lax.axis_size("x")
    return lax.ppermute(block, "x", [(i, (i + distance) % n) for i in range(n)])


def swap(block, axis):
    return lax.ppermute(block, axis, [(0, 1), (1, 0)])


def after(block, *others):
    return lax.optimization_barrier((block, *others))[0] if others else block


class Gather:
    OFFSETS = [(0, 0), (1, 0), (0, -1), (0, 1), (0, 2), (1, -1), (1, 1), (1, 2)]

    def __init__(self, block):
        self.block = block

    def cross(self, *others):
        self.far = swap(after(self.block, *others), "zh")

    def first(self, *others):
        block = after(self.block, *others) if others else self.block
        if not others:
            self.far = swap(block, "zh")
        self.right, self.left, self.opposite = (step_x(block, n) for n in (1, -1, 2))
        return self.far, self.right, self.left, self.opposite

    def first_arrived(self):
        return self.far, self.right, self.left, self.opposite

    def second(self, *others):
        if others:
            self.far = after(self.far, *others)
            self.opposite = after(self.opposite, *others)
        self.far_right, self.far_left = step_x(self.far, 1), step_x(self.far, -1)
        self.far_opposite = swap(self.opposite, "zh")
        return self.far_right, self.far_left, self.far_opposite

    def trade(self, *others):
        got = [self.block, self.far, self.right, self.left, self.opposite]
        if others:
            got = lax.optimization_barrier((*got, *others))[: len(got)]
        self.near = [*got, *(swap(b, "core") for b in got)]

    def blocks(self, *others):
        got = [self.far_right, self.far_left, self.far_opposite]
        if others:
            got = lax.optimization_barrier((*got, *others))[: len(got)]
        got = [*got, *(swap(b, "core") for b in got)]
        return self.near[:5] + got[:3] + self.near[5:] + got[3:]


def turn_kernel(x_ref, o_ref):
    for i in range(x_ref.shape[1] // D):
        o_ref[i * D : (i + 1) * D, :] = x_ref[:, i * D : (i + 1) * D].T


def turn_call(x):
    return pl.pallas_call(
        turn_kernel, out_shape=jax.ShapeDtypeStruct(x.shape[::-1], x.dtype), name="turn"
    )(x)


def route_kernel(table, *rest):
    blocks, mass_refs = rest[:BLOCKS], rest[BLOCKS:-3]
    out_ref, named, sem = rest[-3:]
    for b in range(BLOCKS):
        pltpu.make_async_copy(
            blocks[b].at[pl.ds(blocks[b].shape[0] - EXTRA, EXTRA), pl.ds(0, D)],
            named.at[table[SRC + b]],
            sem,
        ).start()
    pltpu.make_async_copy(named, named, sem).wait()
    own = jnp.concatenate(
        [named[s, 0:1, :].astype(jnp.float32) for s in range(BLOCKS)], axis=0
    )
    lane = lax.broadcasted_iota(jnp.int32, own.shape, 1)
    slot = jnp.zeros_like(own)
    for r in range(16):
        same = own == jnp.broadcast_to(own[:, r : r + 1], own.shape)
        slot = slot + jnp.where(same & (lane > r), 1.0, 0.0)
    wanted = (own * CAP + slot)[:, :16]
    wanted = jnp.concatenate([wanted] * 3, axis=1)
    place = lax.broadcasted_iota(jnp.int32, (32, 48), 0).astype(jnp.float32)
    for s in range(BLOCKS):
        pick = jnp.where(wanted[s : s + 1] == place, 1.0, 0.0).astype(jnp.bfloat16)
        rows = jnp.concatenate(
            [ref[:, 2 * s + p, :] for p in range(2) for ref in mass_refs], axis=0
        ) * (1.0 / REPEAT)
        high = rows.astype(jnp.bfloat16)
        left = rows - high.astype(jnp.float32)
        middle = left.astype(jnp.bfloat16)
        low = (left - middle.astype(jnp.float32)).astype(jnp.bfloat16)
        out = matmul(pick, jnp.concatenate([high, middle, low], axis=0))
        out_ref[:, s] = out.reshape(8, CAP, D)


def route_call(masses, kblocks, table):
    grid_spec = pltpu.PrefetchScalarGridSpec(
        num_scalar_prefetch=1,
        grid=(1,),
        in_specs=[pl.BlockSpec(memory_space=pl.ANY)] * BLOCKS
        + [pl.BlockSpec(m.shape, lambda i, *_: (0, 0, 0)) for m in masses],
        out_specs=pl.BlockSpec((8, BLOCKS, CAP, D), lambda i, *_: (0, 0, 0, 0)),
        scratch_shapes=[
            pltpu.VMEM((BLOCKS, 16, D), jnp.bfloat16),
            pltpu.SemaphoreType.DMA,
        ],
    )
    return pl.pallas_call(
        route_kernel,
        grid_spec=grid_spec,
        out_shape=jax.ShapeDtypeStruct((8, BLOCKS, CAP, D), jnp.float32),
        compiler_params=pltpu.CompilerParams(vmem_limit_bytes=VMEM << 20),
        name="route",
    )(table, *kblocks, *masses)


def body(queries, keys, values, block_mask, counts, owners):
    kv_heads = keys.shape[2] // D
    q, k, v = queries[0], keys[0], values[0]
    zh, x, core = lax.axis_index("zh"), lax.axis_index("x"), lax.axis_index("core")
    me = zh * 8 + x * 2 + core

    extra = jnp.pad(
        owners.reshape(1, 2 * kv_heads).astype(jnp.bfloat16),
        ((0, EXTRA - 1), (0, k.shape[1] - 2 * kv_heads)),
    )
    kg = Gather(jnp.concatenate([k, extra], axis=0))

    query_pass = me * 2 + jnp.arange(2, dtype=jnp.int32)
    key_pass = jnp.arange(PASSAGES, dtype=jnp.int32)
    live = counts[0]
    allowed = (query_pass[:, None] == key_pass) | (
        (block_mask[0] == 1) & (query_pass < live)[:, None] & (key_pass < live)
    )
    place = jnp.cumsum(allowed.astype(jnp.int32), axis=1) - 1
    real = jnp.sum(allowed.astype(jnp.int32), axis=1)
    hit = allowed[:, None, :] & (place[:, None, :] == key_pass[None, :, None])
    idx = jnp.sum(jnp.where(hit, key_pass, 0), axis=2).astype(jnp.int32)
    cnt = (real + 3) // 4 * 4
    src = jnp.stack(
        [
            ((zh + a) % 2) * 8 + ((x + b) % 4) * 2 + (core + c) % 2
            for c in range(2)
            for a, b in Gather.OFFSETS
        ]
    ).astype(jnp.int32)
    planes = jnp.stack([zh, 1 - zh]).astype(jnp.int32)
    pad = jnp.zeros((SRC - FAR - 2,), jnp.int32)
    table = jnp.concatenate([idx.reshape(-1), real, cnt, query_pass, planes, pad, src])

    kg.first()
    vt = turn_call(v)
    vg = Gather(vt)
    arrived = kg.second(table, vt)
    vg.cross(kg.far)
    vg.first(arrived[0])

    kg.trade()
    kblocks = kg.blocks()
    parts, lo = [], 0
    for n in CALLS:
        parts.append(weights_call(after(q, *parts[-1][1:2]) if parts else q, kblocks, table, lo, lo, n))
        lo += n
        if len(parts) == 1:
            vg.second(parts[-1][1])

    owner_count = lax.axis_size("grp")
    outgoing = route_call([p[2] for p in parts], kblocks, table).reshape(
        owner_count * BLOCKS, CAP, D
    )
    vg.trade(outgoing)
    vblocks = vg.blocks(outgoing)
    incoming = lax.all_to_all(outgoing, ("grp",) + SEQ, split_axis=0, concat_axis=0, tiled=True)
    attended = attend_call(vblocks, [p[0] for p in parts], [p[1] for p in parts], table)
    incoming, attended = lax.optimization_barrier((incoming, attended))
    feedback = jnp.sum(incoming.reshape(owner_count, BLOCKS, CAP, D), axis=1)
    return attended[None], feedback[None, None]


def solution(mesh):
    fine = Mesh(mesh.devices.reshape(-1, 2, 4, 2), ("grp",) + SEQ)
    rows = P("grp", SEQ, None)
    in_specs = (rows, rows, rows, rows, P("grp"), P("grp", SEQ, None, None))
    out_specs = (rows, P("grp", SEQ, None, None, None))
    return jax.shard_map(
        body, mesh=fine, in_specs=in_specs, out_specs=out_specs, check_vma=False
    )
```

```python
import functools
import math

import jax
import jax.numpy as jnp
from jax import lax
from jax.experimental import pallas as pl
from jax.experimental.pallas import tpu as pltpu
from jax.sharding import Mesh, PartitionSpec as P

D = 128
PASSAGES = 32
BLOCKS = 16
CAP = 4
REPEAT = 4
WIDE = REPEAT * D
SCALE2 = (D**-0.5) * math.log2(math.e)
LARGE = 2.0**80
SEQ = ("zh", "x", "core")
REAL, COUNT, OWN, FAR, SRC = 64, 66, 68, 70, 80
CALLS = (5, 3)
EXTRA = 16
VMEM = 56
LEAN = 40


def matmul(a, b):
    return lax.dot_general(a, b, (((1,), (0,)), ((), ())), preferred_element_type=jnp.float32)


def rows_at(i, n=1):
    return pl.ds(pl.multiple_of(i * D, D), n * D)


def each(n, body, start=0):
    def step(i, carry):
        body(i)
        return carry

    lax.fori_loop(start, n, step, 0)


def chunks(n, body):
    each(n // 16, lambda i: body(i * 16, 16))

    @pl.when(n % 16 >= 8)
    def _():
        body(n // 16 * 16, 8)

    @pl.when(n % 8 > 0)
    def _():
        body(n // 8 * 8, 4)


def weights_kernel(heads, offset, table, q_ref, *rest):
    kblocks = rest[:BLOCKS]
    p_ref, inv_ref, mass_ref, kbuf, pbuf, qt, total, ksem, psem = rest[BLOCKS:]
    h = pl.program_id(0)

    def whole(cols, i):
        return pltpu.make_async_copy(kbuf.at[:, cols], kbuf.at[:, cols], ksem.at[i])

    spans = [pl.ds(0, D), pl.ds(D, (heads - 1) * D)][: min(heads, 2)]

    @pl.when(h == 0)
    def _():
        for i, cols in enumerate(spans):
            for b in range(BLOCKS):
                pltpu.make_async_copy(
                    kblocks[b].at[pl.ds(0, 2 * D), pl.ds(offset * D + cols.start, cols.size)],
                    kbuf.at[rows_at(table[SRC + b] * 2, 2), cols],
                    ksem.at[i],
                ).start()
        whole(spans[0], 0).wait()

    if heads > 1:

        @pl.when(h == 1)
        def _():
            whole(spans[1], 1).wait()

    mine = pl.ds(pl.multiple_of(h * D, D), D)
    mass_ref[...] = jnp.zeros_like(mass_ref)

    def pcopy(hh, qp, i):
        slot = lax.rem(hh, 2)
        return pltpu.make_async_copy(
            pbuf.at[slot, qp, rows_at(i * 4, 4)],
            p_ref.at[hh, qp, rows_at(i * 4, 4)],
            psem.at[slot, qp, i],
        )

    counts = [table[COUNT + qp] for qp in range(2)]

    mine_p = pbuf.at[lax.rem(h, 2)]

    def drain(hh):
        for qp in range(2):
            each(counts[qp] // 4, lambda i: pcopy(hh, qp, i).wait())

    @pl.when(h > 1)
    def _():
        drain(h - 2)

    def key_at(qp, i):
        return kbuf[rows_at(table[qp * PASSAGES + i]), mine]

    def fill(qp, top):
        def part(first, count):
            k = jnp.concatenate([key_at(qp, first + u) for u in range(count)], axis=0)
            s = matmul(k, qt[qp]) * SCALE2
            acc = total[qp]
            for u in range(count):
                unused = jnp.where(first + u < table[REAL + qp], 0.0, 1e30)
                w = jnp.exp2(s[u * D : (u + 1) * D] - (top + unused))
                mine_p[qp, rows_at(first + u), :] = w.astype(jnp.bfloat16)
                acc = acc + jnp.sum(w.reshape(D // 8, 8, WIDE), axis=0)
            total[qp] = acc
            for u in range(0, count, 4):
                pcopy(h, qp, (first + u) // 4).start()

        total[qp] = jnp.zeros((8, WIDE), jnp.float32)
        chunks(counts[qp], part)

    def summed(qp):
        return jnp.broadcast_to(jnp.sum(total[qp], axis=0, keepdims=True), (8, WIDE))

    for qp in range(2):
        for r in range(REPEAT):
            qt[qp, :, r * D : (r + 1) * D] = q_ref[qp * D : (qp + 1) * D, r * D : (r + 1) * D].T
    own = [
        jnp.max(
            matmul(kbuf[rows_at(table[OWN + qp]), mine], qt[qp]), axis=0, keepdims=True
        )
        for qp in range(2)
    ]
    for qp in range(2):
        fill(qp, own[qp] * SCALE2)

    @pl.when(jnp.max(jnp.maximum(summed(0), summed(1))) > LARGE)
    def _():
        drain(h)
        for qp in range(2):

            def higher(i, top):
                return jnp.maximum(
                    top, jnp.max(matmul(key_at(qp, i), qt[qp]), axis=0, keepdims=True)
                )

            fill(qp, lax.fori_loop(0, counts[qp], higher, own[qp]) * SCALE2)

    invs = [1.0 / summed(qp) for qp in range(2)]
    for qp in range(2):
        inv_ref[0, qp] = invs[qp]

        def mass_part(first, count):
            w = mine_p[qp, rows_at(first, count), :].astype(jnp.float32) * invs[qp][0:1]
            w = w[:, :D] + w[:, D : 2 * D] + w[:, 2 * D : 3 * D] + w[:, 3 * D :]
            for u in range(count):
                row = jnp.sum(w[u * D : (u + 1) * D].T, axis=0, keepdims=True)
                j = table[qp * PASSAGES + first + u]
                mass_ref[0, pl.ds(j, 1), :] += row

        chunks(counts[qp], mass_part)

    @pl.when(h == heads - 1)
    def _():
        if heads > 1:
            drain(h - 1)
        drain(h)


def weights_call(q, kblocks, table, first_head, offset, heads):
    grid_spec = pltpu.PrefetchScalarGridSpec(
        num_scalar_prefetch=1,
        grid=(heads,),
        in_specs=[pl.BlockSpec((2 * D, WIDE), lambda h, *_: (0, h + first_head))]
        + [pl.BlockSpec(memory_space=pl.ANY)] * BLOCKS,
        out_specs=[
            pl.BlockSpec(memory_space=pl.ANY),
            pl.BlockSpec((1, 2, 8, WIDE), lambda h, *_: (h, 0, 0, 0)),
            pl.BlockSpec((1, PASSAGES, D), lambda h, *_: (h, 0, 0)),
        ],
        scratch_shapes=[
            pltpu.VMEM((PASSAGES * D, heads * D), jnp.bfloat16),
            pltpu.VMEM((2, 2, PASSAGES * D, WIDE), jnp.bfloat16),
            pltpu.VMEM((2, D, WIDE), jnp.bfloat16),
            pltpu.VMEM((2, 8, WIDE), jnp.float32),
            pltpu.SemaphoreType.DMA((2,)),
            pltpu.SemaphoreType.DMA((2, 2, PASSAGES // 4)),
        ],
    )
    return pl.pallas_call(
        functools.partial(weights_kernel, heads, offset),
        grid_spec=grid_spec,
        out_shape=[
            jax.ShapeDtypeStruct((heads, 2, PASSAGES * D, WIDE), jnp.bfloat16),
            jax.ShapeDtypeStruct((heads, 2, 8, WIDE), jnp.float32),
            jax.ShapeDtypeStruct((heads, PASSAGES, D), jnp.float32),
        ],
        compiler_params=pltpu.CompilerParams(vmem_limit_bytes=LEAN << 20),
        cost_estimate=pl.CostEstimate(
            flops=heads * 5_000_000_000, bytes_accessed=heads * 4_000_000, transcendentals=0
        ),
        name="weights",
    )(table, q, *kblocks)


def attend_kernel(heads, table, *rest):
    parts = len(heads)
    total = sum(heads)
    p_refs, inv_refs = rest[:parts], rest[parts : 2 * parts]
    vblocks = rest[2 * parts : 2 * parts + BLOCKS]
    o_ref, vbuf, pbuf, acc, vsem, psem = rest[-6:]
    h = pl.program_id(0)

    def pcopy(ref, hh, qp, i, slot):
        return pltpu.make_async_copy(
            ref.at[hh, qp, rows_at(i * 4, 4)], pbuf.at[slot, qp, rows_at(i * 4, 4)], psem.at[slot, qp, i]
        )

    def fetch(hh, qp, slot):
        lo = 0
        for ref, n in zip(p_refs, heads):

            @pl.when((hh >= lo) & (hh < lo + n))
            def _():
                each(table[COUNT + qp] // 4, lambda i: pcopy(ref, hh - lo, qp, i, slot).start())

            lo += n

    def values(hh):
        rows = pl.ds(pl.multiple_of(hh * D, D), D)
        for b in range(BLOCKS):
            pltpu.make_async_copy(
                vblocks[b].at[rows], vbuf.at[table[SRC + b], rows], vsem.at[hh]
            ).start()

    @pl.when(h == 0)
    def _():
        fetch(0, 0, 0)
        values(0)
        fetch(0, 1, 0)

    slot = lax.rem(h, 2)

    @pl.when(h < total - 1)
    def _():
        fetch(h + 1, 0, 1 - slot)
        values(h + 1)
        fetch(h + 1, 1, 1 - slot)

    mine = pl.ds(pl.multiple_of(h * D, D), D)
    pltpu.make_async_copy(vbuf.at[:, mine], vbuf.at[:, mine], vsem.at[h]).wait()

    def value_at(j):
        return vbuf[j // 2, mine, rows_at(j % 2)]

    for qp in range(2):
        n = table[COUNT + qp]
        acc[...] = jnp.zeros_like(acc)

        def part(first, count):
            for u in range(0, count, 4):
                pcopy(p_refs[0], 0, qp, (first + u) // 4, slot).wait()
            v = jnp.concatenate(
                [value_at(table[qp * PASSAGES + first + u]) for u in range(count)], axis=1
            )
            acc[...] += matmul(v, pbuf[slot, qp, rows_at(first, count), :])

        chunks(n, part)

        lo = heads[0]
        inv = inv_refs[0][0, qp, 0:1, :]
        for ref, n in zip(inv_refs[1:], heads[1:]):
            inv = jnp.where(h >= lo, ref[0, qp, 0:1, :], inv)
            lo += n
        o = acc[...] * inv
        for r in range(REPEAT):
            o_ref[qp * D : (qp + 1) * D, r * D : (r + 1) * D] = (
                o[:, r * D : (r + 1) * D].T.astype(jnp.bfloat16)
            )


def attend_call(vblocks, weights, invs, table):
    heads = tuple(w.shape[0] for w in weights)
    total = sum(heads)
    firsts = [sum(heads[:i]) for i in range(len(heads))]

    def inv_spec(lo, n):
        return pl.BlockSpec((1, 2, 8, WIDE), lambda h, *_: (jnp.clip(h - lo, 0, n - 1), 0, 0, 0))

    grid_spec = pltpu.PrefetchScalarGridSpec(
        num_scalar_prefetch=1,
        grid=(total,),
        in_specs=[pl.BlockSpec(memory_space=pl.ANY)] * len(weights)
        + [inv_spec(lo, n) for lo, n in zip(firsts, heads)]
        + [pl.BlockSpec(memory_space=pl.ANY)] * BLOCKS,
        out_specs=pl.BlockSpec((2 * D, WIDE), lambda h, *_: (0, h)),
        scratch_shapes=[
            pltpu.VMEM((BLOCKS, total * D, 2 * D), jnp.bfloat16),
            pltpu.VMEM((2, 2, PASSAGES * D, WIDE), jnp.bfloat16),
            pltpu.VMEM((D, WIDE), jnp.float32),
            pltpu.SemaphoreType.DMA((total,)),
            pltpu.SemaphoreType.DMA((2, 2, PASSAGES // 4)),
        ],
    )
    return pl.pallas_call(
        functools.partial(attend_kernel, heads),
        grid_spec=grid_spec,
        out_shape=jax.ShapeDtypeStruct((2 * D, total * WIDE), jnp.bfloat16),
        compiler_params=pltpu.CompilerParams(vmem_limit_bytes=VMEM << 20),
        cost_estimate=pl.CostEstimate(
            flops=total * 2_000_000_000, bytes_accessed=total * 4_000_000, transcendentals=0
        ),
        name="attend",
    )(table, *weights, *invs, *vblocks)


def step_x(block, distance):
    n = lax.axis_size("x")
    return lax.ppermute(block, "x", [(i, (i + distance) % n) for i in range(n)])


def swap(block, axis):
    return lax.ppermute(block, axis, [(0, 1), (1, 0)])


def after(block, *others):
    return lax.optimization_barrier((block, *others))[0] if others else block


class Gather:
    OFFSETS = [(0, 0), (1, 0), (0, -1), (0, 1), (0, 2), (1, -1), (1, 1), (1, 2)]

    def __init__(self, block):
        self.block = block

    def cross(self, *others):
        self.far = swap(after(self.block, *others), "zh")

    def first(self, *others):
        block = after(self.block, *others) if others else self.block
        if not others:
            self.far = swap(block, "zh")
        self.right, self.left, self.opposite = (step_x(block, n) for n in (1, -1, 2))
        return self.far, self.right, self.left, self.opposite

    def first_arrived(self):
        return self.far, self.right, self.left, self.opposite

    def second(self, *others):
        if others:
            self.far = after(self.far, *others)
            self.opposite = after(self.opposite, *others)
        self.far_right, self.far_left = step_x(self.far, 1), step_x(self.far, -1)
        self.far_opposite = swap(self.opposite, "zh")
        return self.far_right, self.far_left, self.far_opposite

    def trade(self, *others):
        got = [self.block, self.far, self.right, self.left, self.opposite]
        if others:
            got = lax.optimization_barrier((*got, *others))[: len(got)]
        self.near = [*got, *(swap(b, "core") for b in got)]

    def blocks(self, *others):
        got = [self.far_right, self.far_left, self.far_opposite]
        if others:
            got = lax.optimization_barrier((*got, *others))[: len(got)]
        got = [*got, *(swap(b, "core") for b in got)]
        return self.near[:5] + got[:3] + self.near[5:] + got[3:]


def turn_kernel(x_ref, o_ref):
    for i in range(x_ref.shape[1] // D):
        o_ref[i * D : (i + 1) * D, :] = x_ref[:, i * D : (i + 1) * D].T


def turn_call(x):
    return pl.pallas_call(
        turn_kernel, out_shape=jax.ShapeDtypeStruct(x.shape[::-1], x.dtype), name="turn"
    )(x)


def route_kernel(table, *rest):
    blocks, mass_refs = rest[:BLOCKS], rest[BLOCKS:-3]
    out_ref, named, sem = rest[-3:]
    for b in range(BLOCKS):
        pltpu.make_async_copy(
            blocks[b].at[pl.ds(blocks[b].shape[0] - EXTRA, EXTRA), pl.ds(0, D)],
            named.at[table[SRC + b]],
            sem,
        ).start()
    pltpu.make_async_copy(named, named, sem).wait()
    own = jnp.concatenate(
        [named[s, 0:1, :].astype(jnp.float32) for s in range(BLOCKS)], axis=0
    )
    lane = lax.broadcasted_iota(jnp.int32, own.shape, 1)
    slot = jnp.zeros_like(own)
    for r in range(16):
        same = own == jnp.broadcast_to(own[:, r : r + 1], own.shape)
        slot = slot + jnp.where(same & (lane > r), 1.0, 0.0)
    wanted = (own * CAP + slot)[:, :16]
    wanted = jnp.concatenate([wanted] * 3, axis=1)
    place = lax.broadcasted_iota(jnp.int32, (32, 48), 0).astype(jnp.float32)
    for s in range(BLOCKS):
        pick = jnp.where(wanted[s : s + 1] == place, 1.0, 0.0).astype(jnp.bfloat16)
        rows = jnp.concatenate(
            [ref[:, 2 * s + p, :] for p in range(2) for ref in mass_refs], axis=0
        ) * (1.0 / REPEAT)
        high = rows.astype(jnp.bfloat16)
        left = rows - high.astype(jnp.float32)
        middle = left.astype(jnp.bfloat16)
        low = (left - middle.astype(jnp.float32)).astype(jnp.bfloat16)
        out = matmul(pick, jnp.concatenate([high, middle, low], axis=0))
        out_ref[:, s] = out.reshape(8, CAP, D)


def route_call(masses, kblocks, table):
    grid_spec = pltpu.PrefetchScalarGridSpec(
        num_scalar_prefetch=1,
        grid=(1,),
        in_specs=[pl.BlockSpec(memory_space=pl.ANY)] * BLOCKS
        + [pl.BlockSpec(m.shape, lambda i, *_: (0, 0, 0)) for m in masses],
        out_specs=pl.BlockSpec((8, BLOCKS, CAP, D), lambda i, *_: (0, 0, 0, 0)),
        scratch_shapes=[
            pltpu.VMEM((BLOCKS, 16, D), jnp.bfloat16),
            pltpu.SemaphoreType.DMA,
        ],
    )
    return pl.pallas_call(
        route_kernel,
        grid_spec=grid_spec,
        out_shape=jax.ShapeDtypeStruct((8, BLOCKS, CAP, D), jnp.float32),
        compiler_params=pltpu.CompilerParams(vmem_limit_bytes=LEAN << 20),
        name="route",
    )(table, *kblocks, *masses)


def body(queries, keys, values, block_mask, counts, owners):
    kv_heads = keys.shape[2] // D
    q, k, v = queries[0], keys[0], values[0]
    zh, x, core = lax.axis_index("zh"), lax.axis_index("x"), lax.axis_index("core")
    me = zh * 8 + x * 2 + core

    extra = jnp.pad(
        owners.reshape(1, 2 * kv_heads).astype(jnp.bfloat16),
        ((0, EXTRA - 1), (0, k.shape[1] - 2 * kv_heads)),
    )
    kg = Gather(jnp.concatenate([k, extra], axis=0))

    query_pass = me * 2 + jnp.arange(2, dtype=jnp.int32)
    key_pass = jnp.arange(PASSAGES, dtype=jnp.int32)
    live = counts[0]
    allowed = (query_pass[:, None] == key_pass) | (
        (block_mask[0] == 1) & (query_pass < live)[:, None] & (key_pass < live)
    )
    place = jnp.cumsum(allowed.astype(jnp.int32), axis=1) - 1
    real = jnp.sum(allowed.astype(jnp.int32), axis=1)
    hit = allowed[:, None, :] & (place[:, None, :] == key_pass[None, :, None])
    idx = jnp.sum(jnp.where(hit, key_pass, 0), axis=2).astype(jnp.int32)
    cnt = (real + 3) // 4 * 4
    src = jnp.stack(
        [
            ((zh + a) % 2) * 8 + ((x + b) % 4) * 2 + (core + c) % 2
            for c in range(2)
            for a, b in Gather.OFFSETS
        ]
    ).astype(jnp.int32)
    planes = jnp.stack([zh, 1 - zh]).astype(jnp.int32)
    pad = jnp.zeros((SRC - FAR - 2,), jnp.int32)
    table = jnp.concatenate([idx.reshape(-1), real, cnt, query_pass, planes, pad, src])

    kg.first()
    vt = turn_call(v)
    vg = Gather(vt)
    arrived = kg.second(table, vt)
    vg.cross(kg.far)
    vg.first(arrived[0])

    kg.trade()
    kblocks = kg.blocks()
    parts, lo = [], 0
    for n in CALLS:
        parts.append(weights_call(after(q, *parts[-1][1:2]) if parts else q, kblocks, table, lo, lo, n))
        lo += n
        if len(parts) == 1:
            vg.second(parts[-1][1])

    owner_count = lax.axis_size("grp")
    outgoing = route_call([p[2] for p in parts], kblocks, table).reshape(
        owner_count * BLOCKS, CAP, D
    )
    vg.trade(outgoing)
    vblocks = vg.blocks(outgoing)
    incoming = lax.all_to_all(outgoing, ("grp",) + SEQ, split_axis=0, concat_axis=0, tiled=True)
    attended = attend_call(vblocks, [p[0] for p in parts], [p[1] for p in parts], table)
    incoming, attended = lax.optimization_barrier((incoming, attended))
    feedback = jnp.sum(incoming.reshape(owner_count, BLOCKS, CAP, D), axis=1)
    return attended[None], feedback[None, None]


def solution(mesh):
    fine = Mesh(mesh.devices.reshape(-1, 2, 4, 2), ("grp",) + SEQ)
    rows = P("grp", SEQ, None)
    in_specs = (rows, rows, rows, rows, P("grp"), P("grp", SEQ, None, None))
    out_specs = (rows, P("grp", SEQ, None, None, None))
    return jax.shard_map(
        body, mesh=fine, in_specs=in_specs, out_specs=out_specs, check_vma=False
    )
```
